32 devices in a mesh: grp: 2 (over x), leaf: 16 (over z, y, core).
Axes of the slice: x: 2, y: 2, z: 4, core: 2. Of those that a mesh axis runs over, the one named last changes fastest.
Arguments:
- vectors: bfloat16 [32, 65536], P(None, ('grp', 'leaf')), parts along dimension 1, may hold values from -6 to 6
- leaf_basis: bfloat16 [512, 64, 128], P(('grp', 'leaf')), parts along dimension 0, may hold values from -0.5 to 0.5
- src_factors: bfloat16 [3, 512, 64, 128], P(None, ('grp', 'leaf')), parts along dimension 1, may hold values from -0.5 to 0.5
- src_cross: bfloat16 [512, 64, 128], P(('grp', 'leaf')), parts along dimension 0, may hold values from -0.5 to 0.5
- pair_factors: bfloat16 [4096, 64, 128], P(('grp', 'leaf')), parts along dimension 0, may hold values from -0.1875 to 0.1875
- tgt_cross: bfloat16 [512, 64, 128], P(('grp', 'leaf')), parts along dimension 0, may hold values from -0.5 to 0.5
- tgt_factors: bfloat16 [3, 512, 64, 128], P(None, ('grp', 'leaf')), parts along dimension 1, may hold values from -0.5 to 0.5
- out_basis: bfloat16 [512, 64, 128], P(('grp', 'leaf')), parts along dimension 0, may hold values from -0.75 to 0.75
- src_pairing: int32 [3, 16], replicated, may hold values from 0 to 15, as said below
- tgt_pairing: int32 [3, 16], replicated, may hold values from 0 to 15, as said below
- pair_sources: int32 [4096, 2], P(('grp', 'leaf')), parts along dimension 0, may hold values from 0 to 15
- pair_owner: int32 [4096, 1], P(('grp', 'leaf')), parts along dimension 0, may hold values from 0 to 15; in each aligned block of 128 rows (0 to 127, 128 to 255, ...) at most 16 rows name the same one
- pair_target: int32 [4096], P(('grp', 'leaf')), parts along dimension 0, may hold values from 0 to 15
Outputs:
- potentials: bfloat16 [32, 65536], P(None, ('grp', 'leaf')), parts along dimension 1
The draws below stay inside these ranges and needn't reach their ends.
There are 2 independent parts, one for each index of `grp`. The reference program is written for one: setup_inputs(seed, part) draws one part's arguments, and reference() takes and returns one part's arrays. A program takes and returns all parts, laid end to end along the dimension named above; an argument that names none is the same for every part. Nothing has to cross between parts.
Inputs may be any that keep to these rules, and one draw needn't show every extreme that they name: `src_pairing`: each row pairs the 16 blocks of one device two by two: entry j names the partner of j, whose entry names j. `tgt_pairing`: each row pairs the 16 blocks of one device two by two: entry j names the partner of j, whose entry names j. `pair_owner`: among the 128 interactions of one device no owner appears more than 16 times, and some owner appears exactly 16 times.
All inputs are finite; a program needn't handle non-finite values.
Results may differ from the reference program's by a relative error of at most 0.019.
Values may be sent and summed in bfloat16 or wider, within the bound.
A program may use at most 64 MiB of HBM per device.

```python
import math
import jax
import jax.numpy as jnp
import numpy as np
from jax import lax

VECS = 32
RANK = 64
BLK = 128
SB_DEV = 16
LEVELS = 3
PAIR_FAN = 8
PAIRS_DEV = 128
CAP = 16
NSB = 256
NPAIRS = 2048
NPTS = 32768
N_LEAF = 16


def pairing(key):
    orders = jax.vmap(lambda single: jax.random.permutation(single, SB_DEV))(jax.random.split(key, LEVELS)).astype(jnp.int32)
    evens = orders[:, 0::2]
    odds = orders[:, 1::2]
    rows = jnp.arange(LEVELS, dtype=jnp.int32)[:, None]
    partner = jnp.zeros((LEVELS, SB_DEV), jnp.int32)
    partner = partner.at[rows, evens].set(odds)
    partner = partner.at[rows, odds].set(evens)
    return partner


def draw_src_pairing(key, part):
    key = jax.random.fold_in(key, 11)
    return pairing(key)


def draw_tgt_pairing(key, part):
    key = jax.random.fold_in(key, 23)
    return pairing(key)


def place_ends(drawn, key, least, largest):
    dims = drawn.shape
    spot = [jax.random.randint(jax.random.fold_in(key, axis), (), 0, dims[axis]) for axis in range(len(dims))]
    drawn = drawn.at[tuple(spot)].set(least)
    longest = dims.index(max(dims))
    spot[longest] = (spot[longest] + 1) % dims[longest]
    return drawn.at[tuple(spot)].set(largest)


def level_of(stream_key, shape, cuts, low, largest):
    loudness, own = 1.0, jax.random.fold_in(stream_key, 6)
    for position, blocks in cuts:
        steps = jnp.exp(jax.random.uniform(jax.random.fold_in(own, position), (blocks,), jnp.float32, low / len(cuts), largest / len(cuts)))
        loudness = loudness * jnp.repeat(steps, shape[position] // blocks).reshape([-1 if axis == position else 1 for axis in range(len(shape))])
    return loudness


def shared_out(own_key, own, number, rows, count, top, bound, skew):
    ranking = jax.random.permutation(own_key, count)
    packed, common = portions_of(count, rows * top, bound, skew, True), portions_of(count, rows * top, bound, skew, False)
    places = jnp.arange(count)

    def named(lengths, turn):
        used = int((lengths > 0).sum())
        fixed = max(1, used // 4)
        moved = fixed + (places - fixed + turn * (used - fixed)) % max(1, count - fixed)
        return jnp.zeros((count,), jnp.int32).at[ranking[jnp.where(places < fixed, places, moved)]].set(jnp.asarray(lengths, jnp.int32))

    lengths = jnp.where(number % 4 == 0, named(packed, number // 4), named(common, number - number // 4 - 1))
    mixed = jax.random.permutation(jax.random.fold_in(own, 3), count)
    giver, sink = mixed[0:count // 2 * 2:2], mixed[1:count // 2 * 2:2]
    margin = jnp.minimum(lengths[giver] - 1, bound - lengths[sink]) // 2
    margin = jnp.where((giver == ranking[0]) | (sink == ranking[0]) | (lengths[sink] == 0), 0, jnp.maximum(margin, 0))
    moved = jax.random.randint(jax.random.fold_in(own, 4), (count // 2,), 0, 1 << 20) % (margin + 1)
    lengths = lengths.at[giver].add(-moved).at[sink].add(moved)
    items = jnp.searchsorted(jnp.cumsum(lengths), jnp.arange(rows * top), side="right").astype(jnp.int32)
    listing = items.reshape(top, rows).T
    listing = listing[jax.random.permutation(jax.random.fold_in(own, 1), rows)]
    turn = jax.random.randint(jax.random.fold_in(own, 2), (rows, 1), 0, top)
    return jnp.take_along_axis(listing, (jnp.arange(top)[None, :] + turn) % top, axis=1)


def portions_of(amount, total, limit, skew, full):
    portions = [(1 << 20) // math.isqrt(rank ** skew) + 1 for rank in range(1, amount + 1)]
    largest = limit if full else min(limit, max(-(-total // amount), total * portions[0] // sum(portions)))
    least = 1 if total - largest >= amount - 1 else 0
    given, surplus = [largest] + [least] * (amount - 1), total - largest - least * (amount - 1)
    while surplus > 0:
        candidates = [i for i in range(1, amount) if given[i] < largest] or [i for i in range(1, amount) if given[i] < limit]
        whole, left = sum([portions[i] for i in candidates]), surplus
        for i in candidates:
            extra = min(limit - given[i], max(1, left * portions[i] // whole), surplus)
            given[i] = given[i] + extra
            surplus = surplus - extra
    return np.array(given)


def bell_draw(rng, extent, deviation, most, cuts=(), kind=jnp.bfloat16):
    level = level_of(rng, extent, cuts, -0.22, 0.18) if cuts else 1.0
    array = jax.random.normal(rng, extent, jnp.float32) * deviation * level
    return jnp.minimum(jnp.maximum(array, -most), most).astype(kind)


def setup_inputs(seed: int = 0, part: int = 0) -> dict:
    key_of = jax.random.split(jax.random.key(seed), 14)
    own_keys = jax.random.split(jax.random.fold_in(key_of[13], part), 14)
    vectors = bell_draw(own_keys[0], (VECS, NPTS), 1.0, 6.0, ((1, 16),))
    leaf_basis = bell_draw(own_keys[1], (NSB, RANK, BLK), BLK ** -0.5, 0.5, ((0, 16),))
    src_factors = bell_draw(own_keys[2], (LEVELS, NSB, RANK, 2 * RANK), (2 * RANK) ** -0.5, 0.5, ((1, 16),))
    src_cross = bell_draw(own_keys[3], (NSB, RANK, 2 * RANK), (2 * RANK) ** -0.5, 0.5, ((0, 16),))
    pair_factors = bell_draw(own_keys[4], (NPAIRS, RANK, 2 * RANK), (2 * RANK * PAIR_FAN) ** -0.5, 0.1875, ((0, 16),))
    tgt_cross = bell_draw(own_keys[5], (NSB, RANK, 2 * RANK), (2 * RANK) ** -0.5, 0.5, ((0, 16),))
    tgt_factors = bell_draw(own_keys[6], (LEVELS, NSB, RANK, 2 * RANK), (2 * RANK) ** -0.5, 0.5, ((1, 16),))
    out_basis = bell_draw(own_keys[7], (NSB, RANK, BLK), RANK ** -0.5, 0.75, ((0, 16),))
    src_pairing = draw_src_pairing(jax.random.fold_in(key_of[13], 71), part)
    tgt_pairing = draw_tgt_pairing(jax.random.fold_in(key_of[13], 71), part)
    pair_sources = place_ends(jax.random.randint(own_keys[10], (NPAIRS, 2), 0, SB_DEV), jax.random.fold_in(own_keys[10], 1), 0, SB_DEV - 1).astype(jnp.int32)
    pair_owner_keys = jax.random.split(jax.random.fold_in(own_keys[11], 1), NPAIRS // PAIRS_DEV)
    pair_owner_turns = jax.random.permutation(jax.random.fold_in(own_keys[11], 3), NPAIRS // PAIRS_DEV)
    pair_owner = jax.vmap(lambda own, number: shared_out(jax.random.fold_in(own_keys[11], 2), own, number, PAIRS_DEV, N_LEAF, 1, CAP, 2))(pair_owner_keys, pair_owner_turns).reshape((NPAIRS, 1))
    pair_target = place_ends(jax.random.randint(own_keys[12], (NPAIRS,), 0, SB_DEV), jax.random.fold_in(own_keys[12], 1), 0, SB_DEV - 1).astype(jnp.int32)
    return dict(vectors=vectors, leaf_basis=leaf_basis, src_factors=src_factors, src_cross=src_cross, pair_factors=pair_factors, tgt_cross=tgt_cross, tgt_factors=tgt_factors, out_basis=out_basis, src_pairing=src_pairing, tgt_pairing=tgt_pairing, pair_sources=pair_sources, pair_owner=pair_owner, pair_target=pair_target)


def apply_level(factors, current, partner):
    joined = jnp.concatenate([current, current[partner]], axis=1).astype(jnp.float32)
    return jnp.einsum('brk,bkv->brv', factors.astype(jnp.float32), joined).astype(jnp.bfloat16)


def reference(vectors, leaf_basis, src_factors, src_cross, pair_factors, tgt_cross, tgt_factors, out_basis, src_pairing, tgt_pairing, pair_sources, pair_owner, pair_target):
    blocks = jnp.arange(NSB, dtype=jnp.int32)
    block_base = (blocks // SB_DEV) * SB_DEV
    local_index = blocks % SB_DEV
    columns = vectors.reshape(VECS, NSB, BLK).astype(jnp.float32)
    current = jnp.einsum('brk,vbk->brv', leaf_basis.astype(jnp.float32), columns).astype(jnp.bfloat16)
    for depth in range(LEVELS):
        current = apply_level(src_factors[depth], current, block_base + src_pairing[depth][local_index])
    current = apply_level(src_cross, current, (blocks + NSB // 2) % NSB)
    pair_dev = jnp.arange(NPAIRS, dtype=jnp.int32) // PAIRS_DEV
    first_src = pair_dev * SB_DEV + pair_sources[:, 0]
    second_src = pair_dev * SB_DEV + pair_sources[:, 1]
    target = pair_owner[:, 0] * SB_DEV + pair_target
    source_state = current

    def middle(carry, items):
        factors, first_one, second_one, target_one = items
        joined = jnp.concatenate([source_state[first_one], source_state[second_one]], axis=1).astype(jnp.float32)
        results = jnp.einsum('prk,pkv->prv', factors.astype(jnp.float32), joined).astype(jnp.bfloat16)
        results = lax.optimization_barrier(results).astype(jnp.float32)
        return carry + jax.ops.segment_sum(results, target_one, num_segments=NSB), None

    totals = jnp.zeros((NSB, RANK, VECS), jnp.float32)
    totals, unused = lax.scan(middle, totals, (pair_factors.reshape(N_LEAF, PAIRS_DEV, RANK, 2 * RANK), first_src.reshape(N_LEAF, PAIRS_DEV), second_src.reshape(N_LEAF, PAIRS_DEV), target.reshape(N_LEAF, PAIRS_DEV)))
    current = totals.astype(jnp.bfloat16)
    near = jnp.bitwise_xor(blocks // SB_DEV, 1) * SB_DEV + local_index
    current = apply_level(tgt_cross, current, near)
    for depth in range(LEVELS):
        current = apply_level(tgt_factors[depth], current, block_base + tgt_pairing[depth][local_index])
    output = jnp.einsum('brv,brk->vbk', current.astype(jnp.float32), out_basis.astype(jnp.float32))
    return output.reshape(VECS, NPTS).astype(jnp.bfloat16)
```

```python
import functools

import jax
import jax.numpy as jnp
from jax import lax
from jax.experimental import pallas as pl
from jax.experimental.pallas import tpu as pltpu
from jax.sharding import PartitionSpec as P

BF16 = jnp.bfloat16
F32 = jnp.float32
I32 = jnp.int32
NT = (((1,), (1,)), ((), ()))


def bit_of(number, bit):
    return (number // (1 << bit)) % 2


def flip(number, bit):
    return number + (1 << bit) - 2 * (1 << bit) * bit_of(number, bit)


def kernel(
    devices,
    order_of_bits,
    src_pair,
    tgt_pair,
    sources,
    owner,
    target,
    vectors_hbm,
    leaf_hbm,
    src_hbm,
    src_cross_hbm,
    pair_hbm,
    tgt_cross_hbm,
    tgt_hbm,
    out_basis_hbm,
    out_ref,
    vectors,
    leaf,
    src,
    src_cross,
    pair,
    tgt_cross,
    tgt,
    out_basis,
    state_a,
    state_b,
    packed,
    cross_in,
    near_in,
    table_vmem,
    table,
    running,
    dense,
    arrived,
    load_sem,
    table_sem,
    send_sem,
    recv_sem,
):
    me = lax.axis_index("leaf")
    bits = len(order_of_bits)
    blocks = leaf.shape[0]
    halves = blocks // 2
    pairs = pair.shape[0]
    levels = src.shape[0]
    rank = leaf.shape[1]
    vec = vectors.shape[0]
    width = 2 * rank

    loads = [
        pltpu.make_async_copy(hbm, ref, load_sem.at[i])
        for i, (hbm, ref) in enumerate(
            [
                (vectors_hbm, vectors),
                (leaf_hbm, leaf),
                (src_hbm, src),
                (src_cross_hbm, src_cross),
                (pair_hbm, pair),
                (tgt_cross_hbm, tgt_cross),
                (tgt_hbm, tgt),
                (out_basis_hbm, out_basis),
            ]
        )
    ]
    for load in loads:
        load.start()

    barrier = pltpu.get_barrier_semaphore()
    for bit in range(bits):
        pl.semaphore_signal(
            barrier,
            inc=1,
            device_id={"leaf": flip(me, bit)},
            device_id_type=pl.DeviceIdType.MESH,
        )

    def send(source, destination, bit, slot):
        return pltpu.make_async_remote_copy(
            src_ref=source,
            dst_ref=destination,
            send_sem=send_sem.at[slot],
            recv_sem=recv_sem.at[slot],
            device_id={"leaf": flip(me, bit)},
            device_id_type=pl.DeviceIdType.MESH,
        )

    low = lax.broadcasted_iota(I32, (vec, width), 1) < rank

    def twice(x, factor):
        both = jnp.concatenate([factor, factor], axis=0)
        return lax.dot_general(x, both, NT, preferred_element_type=F32)

    def local_level(factors, depth, pairing, old, new):
        for b in range(blocks):
            x = jnp.where(low, old[b], old[pairing[depth, b]])
            new[b] = twice(x, factors[depth, b]).astype(BF16)

    def cross_level(factors, own, other, new):
        for b in range(blocks):
            if b % 2 == 0:
                x = jnp.where(low, other[b // 2], own[b])
                x = jnp.concatenate([x[:, rank:], x[:, :rank]], axis=1)
            else:
                x = jnp.where(low, own[b], other[b // 2])
            new[b] = twice(x, factors[b]).astype(BF16)

    loads[0].wait()
    loads[1].wait()
    points = leaf.shape[2]
    for b in range(blocks):
        state_a[b] = twice(vectors[:, b * points : (b + 1) * points], leaf[b]).astype(BF16)
    loads[2].wait()
    now, later = state_a, state_b
    for depth in range(levels):
        local_level(src, depth, src_pair, now, later)
        now, later = later, now

    for j in range(halves):
        packed[j] = jnp.where(low, now[2 * j], now[2 * j + 1])
    pl.semaphore_wait(barrier, bits)
    cross = send(packed, cross_in, bits - 1, 0)
    cross.start()

    count_shape = (pairs, pairs)
    item = lax.broadcasted_iota(I32, count_shape, 0)
    lane = lax.broadcasted_iota(I32, count_shape, 1)
    key = jnp.broadcast_to(owner[...] * blocks + target[...], count_shape)
    first = jnp.broadcast_to(sources[:, 0:1], count_shape)
    second = jnp.broadcast_to(sources[:, 1:2], count_shape)
    key_row = jnp.sum(jnp.where(item == lane, key, 0), axis=0, keepdims=True)
    before = jnp.where((key_row == key) & (lane < item), 1, 0)
    smaller = jnp.where(key_row < key, 1, 0)
    place = jnp.sum(before + smaller, axis=1, keepdims=True)
    follows = jnp.minimum(jnp.sum(before, axis=1, keepdims=True), 1)
    sits = place == lane
    rows = [
        jnp.sum(jnp.where(sits, value, 0), axis=0, keepdims=True)
        for value in (item, first, second, jnp.broadcast_to(follows, count_shape))
    ]
    for r in range(4):
        table_vmem[r : r + 1, :] = rows[r]
    for r in range(devices * blocks // pairs):
        spot = lane + r * pairs
        upto = jnp.sum(jnp.where(key <= spot, 1, 0), axis=0, keepdims=True)
        under = jnp.sum(jnp.where(key < spot, 1, 0), axis=0, keepdims=True)
        table_vmem[4 + r : 5 + r, :] = jnp.where(upto > under, upto - 1, pairs)
    for r in range(4 + devices * blocks // pairs, table_vmem.shape[0]):
        table_vmem[r : r + 1, :] = jnp.zeros((1, pairs), I32)
    to_scalars = pltpu.make_async_copy(table_vmem, table, table_sem)
    to_scalars.start()
    running[pairs] = jnp.zeros((vec, width), BF16)
    loads[3].wait()
    loads[4].wait()
    to_scalars.wait()

    cross.wait()
    cross_level(src_cross, now, cross_in, later)
    now, later = later, now

    group = 16

    def interactions(step, total):
        for k in range(group):
            i = step * group + k
            x = jnp.where(low, now[table[1, i]], now[table[2, i]])
            c = twice(x, pair[table[0, i]]).astype(BF16).astype(F32)
            total = total * table[3, i].astype(F32) + c
            running[i] = total.astype(BF16)
        return total

    lax.fori_loop(0, pairs // group, interactions, jnp.zeros((vec, width), F32))

    def place_owner(position, carry):
        who = 0
        for s, bit in enumerate(order_of_bits):
            away = bit_of(position, bits - 1 - s)
            who = who + ((bit_of(me, bit) + away) % 2) * (1 << bit)
        start = who * blocks
        row = 4 + start // pairs
        column = start % pairs
        for j in range(halves):
            one = running[table[row, column + 2 * j]]
            two = running[table[row, column + 2 * j + 1]]
            dense[position * halves + j] = jnp.where(low, one, two)
        return carry

    lax.fori_loop(0, devices, place_owner, 0)

    unit = 8
    for s, bit in enumerate(order_of_bits):
        size = (devices >> (s + 1)) * halves
        part = arrived.at[size : 2 * size]
        move = send(dense.at[size : 2 * size], part, bit, 1 + s)
        move.start()
        move.wait()

        def add(step, carry):
            for u in range(unit):
                k = step * unit + u
                dense[k] = (dense[k].astype(F32) + arrived[size + k].astype(F32)).astype(BF16)
            return carry

        lax.fori_loop(0, size // unit, add, 0)

    near = send(dense.at[0:halves], near_in, 0, 1 + bits)
    near.start()
    for j in range(halves):
        x = dense[j]
        later[2 * j] = jnp.concatenate([x[:, :rank], x[:, :rank]], axis=1)
        later[2 * j + 1] = jnp.concatenate([x[:, rank:], x[:, rank:]], axis=1)
    now, later = later, now
    loads[5].wait()
    loads[6].wait()
    loads[7].wait()
    near.wait()
    cross_level(tgt_cross, now, near_in, later)
    now, later = later, now
    for depth in range(levels):
        local_level(tgt, depth, tgt_pair, now, later)
        now, later = later, now
    for b in range(blocks):
        y = jnp.dot(now[b][:, :rank], out_basis[b], preferred_element_type=F32)
        out_ref[:, b * points : (b + 1) * points] = y.astype(BF16)


def body(
    devices,
    vectors,
    leaf_basis,
    src_factors,
    src_cross,
    pair_factors,
    tgt_cross,
    tgt_factors,
    out_basis,
    src_pairing,
    tgt_pairing,
    pair_sources,
    pair_owner,
    pair_target,
):
    vec = vectors.shape[0]
    blocks, rank, _ = leaf_basis.shape
    pairs = pair_factors.shape[0]
    bits = devices.bit_length() - 1
    halves = blocks // 2
    width = 2 * rank
    rows = 4 + devices * blocks // pairs
    rows = -(-rows // 8) * 8
    big = [
        vectors,
        leaf_basis,
        src_factors,
        src_cross,
        pair_factors,
        tgt_cross,
        tgt_factors,
        out_basis,
    ]
    vmem = pl.BlockSpec(memory_space=pltpu.VMEM)
    smem = pl.BlockSpec(memory_space=pltpu.SMEM)
    hbm = pl.BlockSpec(memory_space=pl.ANY)
    return pl.pallas_call(
        functools.partial(kernel, devices, tuple(range(bits))),
        out_shape=jax.ShapeDtypeStruct(vectors.shape, BF16),
        in_specs=[smem, smem, vmem, vmem, vmem] + [hbm] * len(big),
        out_specs=vmem,
        scratch_shapes=[pltpu.VMEM(a.shape, a.dtype) for a in big]
        + [
            pltpu.VMEM((blocks, vec, width), BF16),
            pltpu.VMEM((blocks, vec, width), BF16),
            pltpu.VMEM((halves, vec, width), BF16),
            pltpu.VMEM((halves, vec, width), BF16),
            pltpu.VMEM((halves, vec, width), BF16),
            pltpu.VMEM((rows, pairs), I32),
            pltpu.SMEM((rows, pairs), I32),
            pltpu.VMEM((pairs + 1, vec, width), BF16),
            pltpu.VMEM((devices * halves, vec, width), BF16),
            pltpu.VMEM((devices * halves, vec, width), BF16),
            pltpu.SemaphoreType.DMA((len(big),)),
            pltpu.SemaphoreType.DMA,
            pltpu.SemaphoreType.DMA((2 + bits,)),
            pltpu.SemaphoreType.DMA((2 + bits,)),
        ],
        compiler_params=pltpu.CompilerParams(
            collective_id=0, has_side_effects=True, vmem_limit_bytes=48 * 1024 * 1024
        ),
    )(
        src_pairing,
        tgt_pairing,
        pair_sources,
        pair_owner,
        pair_target.reshape(pairs, 1),
        *big,
    )


def solution(mesh):
    in_specs = (
        P(None, ("grp", "leaf")),
        P(("grp", "leaf"), None, None),
        P(None, ("grp", "leaf"), None, None),
        P(("grp", "leaf"), None, None),
        P(("grp", "leaf"), None, None),
        P(("grp", "leaf"), None, None),
        P(None, ("grp", "leaf"), None, None),
        P(("grp", "leaf"), None, None),
        P(),
        P(),
        P(("grp", "leaf"), None),
        P(("grp", "leaf"), None),
        P(("grp", "leaf")),
    )
    out_specs = P(None, ("grp", "leaf"))
    return jax.shard_map(
        functools.partial(body, mesh.shape["leaf"]),
        mesh=mesh,
        in_specs=in_specs,
        out_specs=out_specs,
        check_vma=False,
    )
```

```python
import functools

import jax
import jax.numpy as jnp
from jax import lax
from jax.experimental import pallas as pl
from jax.experimental.pallas import tpu as pltpu
from jax.sharding import PartitionSpec as P

BF16 = jnp.bfloat16
F32 = jnp.float32
I32 = jnp.int32
NT = (((1,), (1,)), ((), ()))


def bit_of(number, bit):
    return (number // (1 << bit)) % 2


def flip(number, bit):
    return number + (1 << bit) - 2 * (1 << bit) * bit_of(number, bit)


def kernel(
    devices,
    orders,
    src_pair_hbm,
    tgt_pair_hbm,
    sources_hbm,
    owner_hbm,
    target_hbm,
    vectors_hbm,
    leaf_hbm,
    src_hbm,
    src_cross_hbm,
    pair_hbm,
    tgt_cross_hbm,
    tgt_hbm,
    out_basis_hbm,
    out_ref,
    src_pair,
    tgt_pair,
    sources,
    owner,
    target,
    vectors,
    leaf,
    src,
    src_cross,
    pair,
    tgt_cross,
    tgt,
    out_basis,
    state_a,
    state_b,
    packed,
    cross_in,
    near_in,
    table_vmem,
    table,
    running,
    dense_a,
    dense_b,
    arrived_a,
    arrived_b,
    load_sem,
    table_sem,
    send_sem,
    recv_sem,
):
    me = lax.axis_index("leaf")
    bits = len(orders[0])
    blocks = leaf.shape[0]
    halves = blocks // 2
    pairs = pair.shape[0]
    levels = src.shape[0]
    rank = leaf.shape[1]
    vec = vectors.shape[0]
    width = 2 * rank

    loads = [
        pltpu.make_async_copy(hbm, ref, load_sem.at[i])
        for i, (hbm, ref) in enumerate(
            [
                (vectors_hbm, vectors),
                (leaf_hbm, leaf),
                (src_pair_hbm, src_pair),
                (src_hbm, src),
                (sources_hbm, sources),
                (owner_hbm, owner),
                (target_hbm, target),
                (tgt_pair_hbm, tgt_pair),
                (src_cross_hbm, src_cross),
                (pair_hbm, pair),
                (tgt_cross_hbm, tgt_cross),
                (tgt_hbm, tgt),
                (out_basis_hbm, out_basis),
            ]
        )
    ]
    for load in loads:
        load.start()

    barrier = pltpu.get_barrier_semaphore()
    for bit in range(bits):
        pl.semaphore_signal(
            barrier,
            inc=1,
            device_id={"leaf": flip(me, bit)},
            device_id_type=pl.DeviceIdType.MESH,
        )

    def send(source, destination, bit, slot):
        return pltpu.make_async_remote_copy(
            src_ref=source,
            dst_ref=destination,
            send_sem=send_sem.at[slot],
            recv_sem=recv_sem.at[slot],
            device_id={"leaf": flip(me, bit)},
            device_id_type=pl.DeviceIdType.MESH,
        )

    low = lax.broadcasted_iota(I32, (vec, width), 1) < rank

    def twice(x, factor):
        both = jnp.concatenate([factor, factor], axis=0)
        return lax.dot_general(x, both, NT, preferred_element_type=F32)

    def local_level(factors, depth, pairing, old, new):
        for b in range(blocks):
            x = jnp.where(low, old[b], old[pairing[depth, b]])
            new[b] = twice(x, factors[depth, b]).astype(BF16)

    def cross_level(factors, own, other, new):
        for b in range(blocks):
            if b % 2 == 0:
                x = jnp.where(low, other[b // 2], own[b])
                x = jnp.concatenate([x[:, rank:], x[:, :rank]], axis=1)
            else:
                x = jnp.where(low, own[b], other[b // 2])
            new[b] = twice(x, factors[b]).astype(BF16)

    loads[0].wait()
    loads[1].wait()
    points = leaf.shape[2]
    for b in range(blocks):
        state_a[b] = twice(vectors[:, b * points : (b + 1) * points], leaf[b]).astype(BF16)
    loads[2].wait()
    loads[3].wait()
    now, later = state_a, state_b
    for depth in range(levels):
        local_level(src, depth, src_pair, now, later)
        now, later = later, now

    for j in range(halves):
        packed[j] = jnp.where(low, now[2 * j], now[2 * j + 1])
    pl.semaphore_wait(barrier, bits)
    cross = send(packed, cross_in, bits - 1, 0)
    cross.start()

    count_shape = (pairs, pairs)
    item = lax.broadcasted_iota(I32, count_shape, 0)
    lane = lax.broadcasted_iota(I32, count_shape, 1)
    for load in loads[4:8]:
        load.wait()
    key_row = owner[...] * blocks + target[...]
    tag_row = (key_row * blocks + sources[0:1, :]) * blocks + sources[1:2, :]
    tag = jnp.sum(jnp.where(item == lane, tag_row, 0), axis=1, keepdims=True)
    tag = jnp.broadcast_to(tag, count_shape)
    key = tag // (blocks * blocks)
    before = jnp.where((key_row == key) & (lane < item), 1, 0)
    smaller = jnp.where(key_row < key, 1, 0)
    place = jnp.sum(before + smaller, axis=1, keepdims=True)
    follows = jnp.minimum(jnp.sum(before, axis=1, keepdims=True), 1)
    sits = place == lane
    fields = [
        jnp.sum(jnp.where(sits, value, 0), axis=0, keepdims=True)
        for value in (item, tag, jnp.broadcast_to(follows, count_shape))
    ]
    rows = [
        fields[0],
        (fields[1] // blocks) % blocks,
        fields[1] % blocks,
        fields[2],
    ]
    for r in range(4):
        table_vmem[r : r + 1, :] = rows[r]
    for r in range(devices * blocks // pairs):
        spot = lane + r * pairs
        upto = jnp.sum(jnp.where(key <= spot, 1, 0), axis=0, keepdims=True)
        under = jnp.sum(jnp.where(key < spot, 1, 0), axis=0, keepdims=True)
        table_vmem[4 + r : 5 + r, :] = jnp.where(upto > under, upto - 1, pairs)
    for r in range(4 + devices * blocks // pairs, table_vmem.shape[0]):
        table_vmem[r : r + 1, :] = jnp.zeros((1, pairs), I32)
    to_scalars = pltpu.make_async_copy(table_vmem, table, table_sem)
    to_scalars.start()
    running[pairs] = jnp.zeros((vec, width), BF16)
    loads[8].wait()
    loads[9].wait()
    to_scalars.wait()

    cross.wait_recv()
    cross_level(src_cross, now, cross_in, later)
    now, later = later, now

    group = 16

    def interactions(step, total):
        for k in range(group):
            i = step * group + k
            x = jnp.where(low, now[table[1, i]], now[table[2, i]])
            c = twice(x, pair[table[0, i]]).astype(BF16).astype(F32)
            total = total * table[3, i].astype(F32) + c
            running[i] = total.astype(BF16)
        return total

    lax.fori_loop(0, pairs // group, interactions, jnp.zeros((vec, width), F32))

    half = vec // 2
    dense = (dense_a, dense_b)
    arrived = (arrived_a, arrived_b)

    def place(h, begin, end):
        part = pl.ds(h * half, half)
        low_half = low[:half]

        def place_owner(position, carry):
            who = 0
            for s, bit in enumerate(orders[h]):
                away = bit_of(position, bits - 1 - s)
                who = who + ((bit_of(me, bit) + away) % 2) * (1 << bit)
            start = who * blocks
            row = 4 + start // pairs
            column = start % pairs
            for j in range(halves):
                one = running[table[row, column + 2 * j], part, :]
                two = running[table[row, column + 2 * j + 1], part, :]
                dense[h][position * halves + j] = jnp.where(low_half, one, two)
            return carry

        lax.fori_loop(begin, end, place_owner, 0)

    unit = 4

    def add(h, offset, begin, end):
        def step_of(step, carry):
            for u in range(unit):
                k = step * unit + u
                total = dense[h][k].astype(F32) + arrived[h][offset + k].astype(F32)
                dense[h][k] = total.astype(BF16)
            return carry

        lax.fori_loop(begin // unit, end // unit, step_of, 0)

    def move_of(h, s):
        size = (devices >> (s + 1)) * halves
        part = pl.ds(size, size)
        slot = 2 + 2 * s + h
        return send(dense[h].at[part], arrived[h].at[part], orders[h][s], slot)

    moves = [[move_of(h, s) for s in range(bits)] for h in range(2)]
    for h in range(2):
        place(h, devices // 2, devices)
        moves[h][0].start()
    for h in range(2):
        place(h, 0, devices // 2)
    for s in range(bits):
        size = (devices >> (s + 1)) * halves
        for h in range(2):
            moves[h][s].wait_recv()
            if s + 1 < bits:
                add(h, size, size // 2, size)
                moves[h][s + 1].start()
                add(h, size, 0, size // 2)
            else:
                add(h, size, 0, size)
    middle = packed
    cross.wait_send()
    for j in range(halves):
        middle[j] = jnp.concatenate([dense_a[j], dense_b[j]], axis=0)

    near = send(middle, near_in, 0, 1)
    near.start()
    for j in range(halves):
        x = middle[j]
        later[2 * j] = jnp.concatenate([x[:, :rank], x[:, :rank]], axis=1)
        later[2 * j + 1] = jnp.concatenate([x[:, rank:], x[:, rank:]], axis=1)
    now, later = later, now
    for load in loads[10:]:
        load.wait()
    near.wait()
    for h in range(2):
        for move in moves[h]:
            move.wait_send()
    cross_level(tgt_cross, now, near_in, later)
    now, later = later, now
    for depth in range(levels):
        local_level(tgt, depth, tgt_pair, now, later)
        now, later = later, now
    for b in range(blocks):
        y = jnp.dot(now[b][:, :rank], out_basis[b], preferred_element_type=F32)
        out_ref[:, b * points : (b + 1) * points] = y.astype(BF16)


def body(
    devices,
    vectors,
    leaf_basis,
    src_factors,
    src_cross,
    pair_factors,
    tgt_cross,
    tgt_factors,
    out_basis,
    src_pairing,
    tgt_pairing,
    pair_sources,
    pair_owner,
    pair_target,
):
    vec = vectors.shape[0]
    blocks, rank, _ = leaf_basis.shape
    pairs = pair_factors.shape[0]
    bits = devices.bit_length() - 1
    halves = blocks // 2
    width = 2 * rank
    rows = 4 + devices * blocks // pairs
    rows = -(-rows // 8) * 8
    small = [
        src_pairing,
        tgt_pairing,
        pair_sources.T,
        pair_owner.reshape(1, pairs),
        pair_target.reshape(1, pairs),
    ]
    big = [
        vectors,
        leaf_basis,
        src_factors,
        src_cross,
        pair_factors,
        tgt_cross,
        tgt_factors,
        out_basis,
    ]
    vmem = pl.BlockSpec(memory_space=pltpu.VMEM)
    hbm = pl.BlockSpec(memory_space=pltpu.HBM)
    rest = list(range(1, bits))
    orders = ([0] + rest, [0] + rest[len(rest) // 2 :] + rest[: len(rest) // 2])
    return pl.pallas_call(
        functools.partial(kernel, devices, orders),
        out_shape=jax.ShapeDtypeStruct(vectors.shape, BF16),
        in_specs=[hbm] * (len(small) + len(big)),
        out_specs=vmem,
        scratch_shapes=[pltpu.SMEM(a.shape, I32) for a in small[:2]]
        + [pltpu.VMEM(a.shape, a.dtype) for a in small[2:] + big]
        + [
            pltpu.VMEM((blocks, vec, width), BF16),
            pltpu.VMEM((blocks, vec, width), BF16),
            pltpu.VMEM((halves, vec, width), BF16),
            pltpu.VMEM((halves, vec, width), BF16),
            pltpu.VMEM((halves, vec, width), BF16),
            pltpu.VMEM((rows, pairs), I32),
            pltpu.SMEM((rows, pairs), I32),
            pltpu.VMEM((pairs + 1, vec, width), BF16),
            pltpu.VMEM((devices * halves, vec // 2, width), BF16),
            pltpu.VMEM((devices * halves, vec // 2, width), BF16),
            pltpu.VMEM((devices * halves, vec // 2, width), BF16),
            pltpu.VMEM((devices * halves, vec // 2, width), BF16),
            pltpu.SemaphoreType.DMA((len(small) + len(big),)),
            pltpu.SemaphoreType.DMA,
            pltpu.SemaphoreType.DMA((2 + 2 * bits,)),
            pltpu.SemaphoreType.DMA((2 + 2 * bits,)),
        ],
        compiler_params=pltpu.CompilerParams(
            collective_id=0, has_side_effects=True, vmem_limit_bytes=63 * 1024 * 1024
        ),
    )(
        *small,
        *big,
    )


def solution(mesh):
    in_specs = (
        P(None, ("grp", "leaf")),
        P(("grp", "leaf"), None, None),
        P(None, ("grp", "leaf"), None, None),
        P(("grp", "leaf"), None, None),
        P(("grp", "leaf"), None, None),
        P(("grp", "leaf"), None, None),
        P(None, ("grp", "leaf"), None, None),
        P(("grp", "leaf"), None, None),
        P(),
        P(),
        P(("grp", "leaf"), None),
        P(("grp", "leaf"), None),
        P(("grp", "leaf")),
    )
    out_specs = P(None, ("grp", "leaf"))
    return jax.shard_map(
        functools.partial(body, mesh.shape["leaf"]),
        mesh=mesh,
        in_specs=in_specs,
        out_specs=out_specs,
        check_vma=False,
    )
```

```python
import functools

import jax
import jax.numpy as jnp
from jax import lax
from jax.experimental import pallas as pl
from jax.experimental.pallas import tpu as pltpu
from jax.sharding import PartitionSpec as P

BF16 = jnp.bfloat16
F32 = jnp.float32
I32 = jnp.int32
NT = (((1,), (1,)), ((), ()))


def bit_of(number, bit):
    return (number // (1 << bit)) % 2


def flip(number, bit):
    return number + (1 << bit) - 2 * (1 << bit) * bit_of(number, bit)


def kernel(
    devices,
    orders,
    src_pair_hbm,
    tgt_pair_hbm,
    sources_hbm,
    owner_hbm,
    target_hbm,
    vectors_hbm,
    leaf_hbm,
    src_hbm,
    src_cross_hbm,
    pair_hbm,
    tgt_cross_hbm,
    tgt_hbm,
    out_basis_hbm,
    out_ref,
    src_pair,
    tgt_pair,
    sources,
    owner,
    target,
    vectors,
    leaf,
    src,
    src_cross,
    pair,
    tgt_cross,
    tgt,
    out_basis,
    state_a,
    state_b,
    packed,
    cross_in,
    near_in,
    table_vmem,
    table,
    running,
    dense_a,
    dense_b,
    arrived_a,
    arrived_b,
    load_sem,
    table_sem,
    send_sem,
    recv_sem,
):
    me = lax.axis_index("leaf")
    bits = len(orders[0])
    blocks = leaf.shape[0]
    halves = blocks // 2
    pairs = pair.shape[0]
    levels = src.shape[0]
    rank = leaf.shape[1]
    vec = vectors.shape[0]
    width = 2 * rank

    loads = [
        pltpu.make_async_copy(hbm, ref, load_sem.at[i])
        for i, (hbm, ref) in enumerate(
            [
                (vectors_hbm, vectors),
                (leaf_hbm, leaf),
                (src_pair_hbm, src_pair),
                (src_hbm, src),
                (sources_hbm, sources),
                (owner_hbm, owner),
                (target_hbm, target),
                (tgt_pair_hbm, tgt_pair),
                (src_cross_hbm, src_cross),
                (pair_hbm, pair),
                (tgt_cross_hbm, tgt_cross),
                (tgt_hbm, tgt),
                (out_basis_hbm, out_basis),
            ]
        )
    ]
    for load in loads:
        load.start()

    barrier = pltpu.get_barrier_semaphore()
    for bit in range(bits):
        pl.semaphore_signal(
            barrier,
            inc=1,
            device_id={"leaf": flip(me, bit)},
            device_id_type=pl.DeviceIdType.MESH,
        )

    def send(source, destination, bit, slot):
        return pltpu.make_async_remote_copy(
            src_ref=source,
            dst_ref=destination,
            send_sem=send_sem.at[slot],
            recv_sem=recv_sem.at[slot],
            device_id={"leaf": flip(me, bit)},
            device_id_type=pl.DeviceIdType.MESH,
        )

    low = lax.broadcasted_iota(I32, (vec, width), 1) < rank

    def times(x, factor):
        return lax.dot_general(x, factor, NT, preferred_element_type=F32)

    def twice(y):
        y = y.astype(BF16)
        return jnp.concatenate([y, y], axis=1)

    def local_level(factors, depth, pairing, old, new):
        for b in range(blocks):
            x = jnp.where(low, old[b], old[pairing[depth, b]])
            new[b] = twice(times(x, factors[depth, b]))

    def cross_level(factors, own, other, new):
        for b in range(blocks):
            if b % 2 == 0:
                x = jnp.where(low, other[b // 2], own[b])
                x = jnp.concatenate([x[:, rank:], x[:, :rank]], axis=1)
            else:
                x = jnp.where(low, own[b], other[b // 2])
            new[b] = twice(times(x, factors[b]))

    loads[0].wait()
    loads[1].wait()
    points = leaf.shape[2]
    for b in range(blocks):
        state_a[b] = twice(times(vectors[:, b * points : (b + 1) * points], leaf[b]))
    loads[2].wait()
    loads[3].wait()
    now, later = state_a, state_b
    for depth in range(levels):
        local_level(src, depth, src_pair, now, later)
        now, later = later, now

    for j in range(halves):
        packed[j] = jnp.where(low, now[2 * j], now[2 * j + 1])
    pl.semaphore_wait(barrier, bits)
    cross = send(packed, cross_in, bits - 1, 0)
    cross.start()

    count_shape = (pairs, pairs)
    item = lax.broadcasted_iota(I32, count_shape, 0)
    lane = lax.broadcasted_iota(I32, count_shape, 1)
    for load in loads[4:8]:
        load.wait()
    key_row = owner[...] * blocks + target[...]
    tag_row = (key_row * blocks + sources[0:1, :]) * blocks + sources[1:2, :]
    tag = jnp.sum(jnp.where(item == lane, tag_row, 0), axis=1, keepdims=True)
    tag = jnp.broadcast_to(tag, count_shape)
    key = tag // (blocks * blocks)
    before = jnp.where((key_row == key) & (lane < item), 1, 0)
    smaller = jnp.where(key_row < key, 1, 0)
    place = jnp.sum(before + smaller, axis=1, keepdims=True)
    follows = jnp.minimum(jnp.sum(before, axis=1, keepdims=True), 1)
    sits = place == lane
    fields = [
        jnp.sum(jnp.where(sits, value, 0), axis=0, keepdims=True)
        for value in (item, tag, jnp.broadcast_to(follows, count_shape))
    ]
    rows = [
        fields[0],
        (fields[1] // blocks) % blocks,
        fields[1] % blocks,
        fields[2],
    ]
    for r in range(4):
        table_vmem[r : r + 1, :] = rows[r]
    for r in range(devices * blocks // pairs):
        spot = lane + r * pairs
        upto = jnp.sum(jnp.where(key <= spot, 1, 0), axis=0, keepdims=True)
        under = jnp.sum(jnp.where(key < spot, 1, 0), axis=0, keepdims=True)
        table_vmem[4 + r : 5 + r, :] = jnp.where(upto > under, upto - 1, pairs)
    for r in range(4 + devices * blocks // pairs, table_vmem.shape[0]):
        table_vmem[r : r + 1, :] = jnp.zeros((1, pairs), I32)
    to_scalars = pltpu.make_async_copy(table_vmem, table, table_sem)
    to_scalars.start()
    running[pairs] = jnp.zeros((vec, width), BF16)
    loads[8].wait()
    loads[9].wait()
    to_scalars.wait()

    cross.wait_recv()
    cross_level(src_cross, now, cross_in, later)
    now, later = later, now

    group = 128

    def interactions(step, total):
        for k in range(group):
            i = step * group + k
            x = jnp.where(low, now[table[1, i]], now[table[2, i]])
            c = times(x, pair[table[0, i]]).astype(BF16).astype(F32)
            total = total * table[3, i].astype(F32) + c
            running[i] = twice(total)
        return total

    lax.fori_loop(0, pairs // group, interactions, jnp.zeros((vec, rank), F32))

    half = vec // 2
    dense = (dense_a, dense_b)
    arrived = (arrived_a, arrived_b)

    def place(begin, end):
        def place_owner(position, carry):
            who, spots = 0, [0, 0]
            for s, bit in enumerate(orders[0]):
                away = bit_of(position, bits - 1 - s)
                who = who + ((bit_of(me, bit) + away) % 2) * (1 << bit)
                for h in range(2):
                    spots[h] += away * (1 << (bits - 1 - orders[h].index(bit)))
            start = who * blocks
            row = 4 + start // pairs
            column = start % pairs
            for j in range(halves):
                one = running[table[row, column + 2 * j]]
                two = running[table[row, column + 2 * j + 1]]
                both = jnp.where(low, one, two)
                dense_a[spots[0] * halves + j] = both[:half]
                dense_b[spots[1] * halves + j] = both[half:]
            return carry

        lax.fori_loop(begin, end, place_owner, 0)

    unit = 4

    def add(h, offset, begin, end):
        def step_of(step, carry):
            for u in range(unit):
                k = step * unit + u
                total = dense[h][k].astype(F32) + arrived[h][offset + k].astype(F32)
                dense[h][k] = total.astype(BF16)
            return carry

        lax.fori_loop(begin // unit, end // unit, step_of, 0)

    def move_of(h, s):
        size = (devices >> (s + 1)) * halves
        part = pl.ds(size, size)
        slot = 2 + 2 * s + h
        return send(dense[h].at[part], arrived[h].at[part], orders[h][s], slot)

    moves = [[move_of(h, s) for s in range(bits)] for h in range(2)]
    place(devices // 2, devices)
    for h in range(2):
        moves[h][0].start()
    place(0, devices // 2)
    for s in range(bits):
        size = (devices >> (s + 1)) * halves
        for h in range(2):
            moves[h][s].wait_recv()
            add(h, size, size // 2 if s + 1 < bits else 0, size)
            if s + 1 < bits:
                moves[h][s + 1].start()
        if s + 1 < bits:
            for h in range(2):
                add(h, size, 0, size // 2)
    middle = packed
    cross.wait_send()
    for j in range(halves):
        middle[j] = jnp.concatenate([dense_a[j], dense_b[j]], axis=0)

    near = send(middle, near_in, 0, 1)
    near.start()
    for j in range(halves):
        x = middle[j]
        later[2 * j] = jnp.concatenate([x[:, :rank], x[:, :rank]], axis=1)
        later[2 * j + 1] = jnp.concatenate([x[:, rank:], x[:, rank:]], axis=1)
    now, later = later, now
    for load in loads[10:]:
        load.wait()
    near.wait()
    for h in range(2):
        for move in moves[h]:
            move.wait_send()
    cross_level(tgt_cross, now, near_in, later)
    now, later = later, now
    for depth in range(levels):
        local_level(tgt, depth, tgt_pair, now, later)
        now, later = later, now
    for b in range(blocks):
        y = jnp.dot(now[b][:, :rank], out_basis[b], preferred_element_type=F32)
        out_ref[:, b * points : (b + 1) * points] = y.astype(BF16)


def body(
    devices,
    vectors,
    leaf_basis,
    src_factors,
    src_cross,
    pair_factors,
    tgt_cross,
    tgt_factors,
    out_basis,
    src_pairing,
    tgt_pairing,
    pair_sources,
    pair_owner,
    pair_target,
):
    vec = vectors.shape[0]
    blocks, rank, _ = leaf_basis.shape
    pairs = pair_factors.shape[0]
    bits = devices.bit_length() - 1
    halves = blocks // 2
    width = 2 * rank
    rows = 4 + devices * blocks // pairs
    rows = -(-rows // 8) * 8
    small = [
        src_pairing,
        tgt_pairing,
        pair_sources.T,
        pair_owner.reshape(1, pairs),
        pair_target.reshape(1, pairs),
    ]
    big = [
        vectors,
        leaf_basis,
        src_factors,
        src_cross,
        pair_factors,
        tgt_cross,
        tgt_factors,
        out_basis,
    ]
    vmem = pl.BlockSpec(memory_space=pltpu.VMEM)
    hbm = pl.BlockSpec(memory_space=pltpu.HBM)
    rest = list(range(1, bits))
    orders = ([0] + rest, [0] + rest[len(rest) // 2 :] + rest[: len(rest) // 2])
    return pl.pallas_call(
        functools.partial(kernel, devices, orders),
        out_shape=jax.ShapeDtypeStruct(vectors.shape, BF16),
        in_specs=[hbm] * (len(small) + len(big)),
        out_specs=vmem,
        scratch_shapes=[pltpu.SMEM(a.shape, I32) for a in small[:2]]
        + [pltpu.VMEM(a.shape, a.dtype) for a in small[2:] + big]
        + [
            pltpu.VMEM((blocks, vec, width), BF16),
            pltpu.VMEM((blocks, vec, width), BF16),
            pltpu.VMEM((halves, vec, width), BF16),
            pltpu.VMEM((halves, vec, width), BF16),
            pltpu.VMEM((halves, vec, width), BF16),
            pltpu.VMEM((rows, pairs), I32),
            pltpu.SMEM((rows, pairs), I32),
            pltpu.VMEM((pairs + 1, vec, width), BF16),
            pltpu.VMEM((devices * halves, vec // 2, width), BF16),
            pltpu.VMEM((devices * halves, vec // 2, width), BF16),
            pltpu.VMEM((devices * halves, vec // 2, width), BF16),
            pltpu.VMEM((devices * halves, vec // 2, width), BF16),
            pltpu.SemaphoreType.DMA((len(small) + len(big),)),
            pltpu.SemaphoreType.DMA,
            pltpu.SemaphoreType.DMA((2 + 2 * bits,)),
            pltpu.SemaphoreType.DMA((2 + 2 * bits,)),
        ],
        compiler_params=pltpu.CompilerParams(
            collective_id=0, has_side_effects=True, vmem_limit_bytes=63 * 1024 * 1024
        ),
    )(
        *small,
        *big,
    )


def solution(mesh):
    in_specs = (
        P(None, ("grp", "leaf")),
        P(("grp", "leaf"), None, None),
        P(None, ("grp", "leaf"), None, None),
        P(("grp", "leaf"), None, None),
        P(("grp", "leaf"), None, None),
        P(("grp", "leaf"), None, None),
        P(None, ("grp", "leaf"), None, None),
        P(("grp", "leaf"), None, None),
        P(),
        P(),
        P(("grp", "leaf"), None),
        P(("grp", "leaf"), None),
        P(("grp", "leaf")),
    )
    out_specs = P(None, ("grp", "leaf"))
    return jax.shard_map(
        functools.partial(body, mesh.shape["leaf"]),
        mesh=mesh,
        in_specs=in_specs,
        out_specs=out_specs,
        check_vma=False,
    )
```

```python
import functools

import jax
import jax.numpy as jnp
from jax import lax
from jax.experimental import pallas as pl
from jax.experimental.pallas import tpu as pltpu
from jax.sharding import PartitionSpec as P

BF16 = jnp.bfloat16
F32 = jnp.float32
I32 = jnp.int32
NT = (((1,), (1,)), ((), ()))


def bit_of(number, bit):
    return (number // (1 << bit)) % 2


def flip(number, bit):
    return number + (1 << bit) - 2 * (1 << bit) * bit_of(number, bit)


def kernel(
    devices,
    orders,
    src_pair_hbm,
    tgt_pair_hbm,
    sources_hbm,
    owner_hbm,
    target_hbm,
    vectors_hbm,
    leaf_hbm,
    src_hbm,
    src_cross_hbm,
    pair_hbm,
    tgt_cross_hbm,
    tgt_hbm,
    out_basis_hbm,
    out_ref,
    src_pair,
    tgt_pair,
    sources,
    owner,
    target,
    vectors,
    leaf,
    src,
    src_cross,
    pair,
    tgt_cross,
    tgt,
    out_basis,
    state_a,
    state_b,
    packed,
    cross_in,
    near_in,
    table_vmem,
    table,
    running,
    dense_a,
    dense_b,
    arrived_a,
    arrived_b,
    load_sem,
    table_sem,
    send_sem,
    recv_sem,
):
    me = lax.axis_index("leaf")
    bits = len(orders[0])
    blocks = leaf.shape[0]
    halves = blocks // 2
    pairs = pair.shape[0]
    levels = src.shape[0]
    rank = leaf.shape[1]
    vec = vectors.shape[0]
    width = 2 * rank

    loads = [
        pltpu.make_async_copy(hbm, ref, load_sem.at[i])
        for i, (hbm, ref) in enumerate(
            [
                (vectors_hbm, vectors),
                (leaf_hbm, leaf),
                (src_pair_hbm, src_pair),
                (src_hbm, src),
                (sources_hbm, sources),
                (owner_hbm, owner),
                (target_hbm, target),
                (tgt_pair_hbm, tgt_pair),
                (src_cross_hbm, src_cross),
                (pair_hbm, pair),
                (tgt_cross_hbm, tgt_cross),
                (tgt_hbm, tgt),
                (out_basis_hbm, out_basis),
            ]
        )
    ]
    for load in loads:
        load.start()

    barrier = pltpu.get_barrier_semaphore()
    for bit in range(bits):
        pl.semaphore_signal(
            barrier,
            inc=1,
            device_id={"leaf": flip(me, bit)},
            device_id_type=pl.DeviceIdType.MESH,
        )

    def send(source, destination, bit, slot):
        return pltpu.make_async_remote_copy(
            src_ref=source,
            dst_ref=destination,
            send_sem=send_sem.at[slot],
            recv_sem=recv_sem.at[slot],
            device_id={"leaf": flip(me, bit)},
            device_id_type=pl.DeviceIdType.MESH,
        )

    low = lax.broadcasted_iota(I32, (vec, width), 1) < rank

    def times(x, factor):
        return lax.dot_general(x, factor, NT, preferred_element_type=F32)

    def twice(y):
        y = y.astype(BF16)
        return jnp.concatenate([y, y], axis=1)

    def local_level(factors, depth, pairing, old, new):
        for b in range(blocks):
            x = jnp.where(low, old[b], old[pairing[depth, b]])
            new[b] = twice(times(x, factors[depth, b]))

    def cross_level(factors, own, other, new):
        for b in range(blocks):
            if b % 2 == 0:
                x = jnp.where(low, other[b // 2], own[b])
                x = jnp.concatenate([x[:, rank:], x[:, :rank]], axis=1)
            else:
                x = jnp.where(low, own[b], other[b // 2])
            new[b] = twice(times(x, factors[b]))

    loads[0].wait()
    loads[1].wait()
    points = leaf.shape[2]
    for b in range(blocks):
        state_a[b] = twice(times(vectors[:, b * points : (b + 1) * points], leaf[b]))
    loads[2].wait()
    loads[3].wait()
    now, later = state_a, state_b
    for depth in range(levels):
        local_level(src, depth, src_pair, now, later)
        now, later = later, now

    for j in range(halves):
        packed[j] = jnp.where(low, now[2 * j], now[2 * j + 1])
    pl.semaphore_wait(barrier, bits)
    cross = send(packed, cross_in, bits - 1, 0)
    cross.start()

    count_shape = (pairs, pairs)
    item = lax.broadcasted_iota(I32, count_shape, 0)
    lane = lax.broadcasted_iota(I32, count_shape, 1)
    for load in loads[4:8]:
        load.wait()
    key_row = owner[...] * blocks + target[...]
    tag_row = (key_row * blocks + sources[0:1, :]) * blocks + sources[1:2, :]
    tag = jnp.sum(jnp.where(item == lane, tag_row, 0), axis=1, keepdims=True)
    tag = jnp.broadcast_to(tag, count_shape)
    key = tag // (blocks * blocks)
    before = jnp.where((key_row == key) & (lane < item), 1, 0)
    smaller = jnp.where(key_row < key, 1, 0)
    place = jnp.sum(before + smaller, axis=1, keepdims=True)
    follows = jnp.minimum(jnp.sum(before, axis=1, keepdims=True), 1)
    sits = place == lane
    fields = [
        jnp.sum(jnp.where(sits, value, 0), axis=0, keepdims=True)
        for value in (item, tag, jnp.broadcast_to(follows, count_shape))
    ]
    rows = [
        fields[0],
        (fields[1] // blocks) % blocks,
        fields[1] % blocks,
        fields[2],
    ]
    for r in range(4):
        table_vmem[r : r + 1, :] = rows[r]
    for r in range(devices * blocks // pairs):
        spot = lane + r * pairs
        upto = jnp.sum(jnp.where(key <= spot, 1, 0), axis=0, keepdims=True)
        under = jnp.sum(jnp.where(key < spot, 1, 0), axis=0, keepdims=True)
        table_vmem[4 + r : 5 + r, :] = jnp.where(upto > under, upto - 1, pairs)
    for r in range(4 + devices * blocks // pairs, table_vmem.shape[0]):
        table_vmem[r : r + 1, :] = jnp.zeros((1, pairs), I32)
    to_scalars = pltpu.make_async_copy(table_vmem, table, table_sem)
    to_scalars.start()
    running[pairs] = jnp.zeros((vec, width), BF16)
    loads[8].wait()
    loads[9].wait()
    to_scalars.wait()

    cross.wait_recv()
    cross_level(src_cross, now, cross_in, later)
    now, later = later, now

    group = 128

    def interactions(step, total):
        for k in range(group):
            i = step * group + k
            x = jnp.where(low, now[table[1, i]], now[table[2, i]])
            c = times(x, pair[table[0, i]]).astype(BF16).astype(F32)
            total = total * table[3, i].astype(F32) + c
            running[i] = twice(total)
        return total

    lax.fori_loop(0, pairs // group, interactions, jnp.zeros((vec, rank), F32))

    half = vec // 2
    dense = (dense_a, dense_b)
    arrived = (arrived_a, arrived_b)

    mine = [bit_of(me, bit) for bit in range(bits)]

    def place(begin, end):
        def place_owner(position, carry):
            who, spots = 0, [0, 0]
            for s, bit in enumerate(orders[0]):
                away = bit_of(position, bits - 1 - s)
                who = who + (mine[bit] + away - 2 * mine[bit] * away) * (1 << bit)
                for h in range(2):
                    spots[h] += away * (1 << (bits - 1 - orders[h].index(bit)))
            start = who * blocks
            row = 4 + start // pairs
            column = start % pairs
            for j in range(halves):
                one = running[table[row, column + 2 * j]]
                two = running[table[row, column + 2 * j + 1]]
                both = jnp.where(low, one, two)
                dense_a[spots[0] * halves + j] = both[:half]
                dense_b[spots[1] * halves + j] = both[half:]
            return carry

        if devices > 16:
            lax.fori_loop(begin, end, place_owner, 0)
        else:
            for position in range(begin, end):
                place_owner(position, 0)

    unit = 4

    def add(h, offset, begin, end):
        def step_of(step, carry):
            for u in range(unit):
                k = step * unit + u
                total = dense[h][k].astype(F32) + arrived[h][offset + k].astype(F32)
                dense[h][k] = total.astype(BF16)
            return carry

        lax.fori_loop(begin // unit, end // unit, step_of, 0)

    def move_of(h, s):
        size = (devices >> (s + 1)) * halves
        part = pl.ds(size, size)
        slot = 2 + 2 * s + h
        return send(dense[h].at[part], arrived[h].at[part], orders[h][s], slot)

    moves = [[move_of(h, s) for s in range(bits)] for h in range(2)]
    place(devices // 2, devices)
    for h in range(2):
        moves[h][0].start()
    place(0, devices // 2)
    for s in range(bits):
        size = (devices >> (s + 1)) * halves
        for h in range(2):
            moves[h][s].wait_recv()
            add(h, size, size // 2 if s + 1 < bits else 0, size)
            if s + 1 < bits:
                moves[h][s + 1].start()
        if s + 1 < bits:
            for h in range(2):
                add(h, size, 0, size // 2)
    middle = packed
    cross.wait_send()
    for j in range(halves):
        middle[j] = jnp.concatenate([dense_a[j], dense_b[j]], axis=0)

    near = send(middle, near_in, 0, 1)
    near.start()
    for j in range(halves):
        x = middle[j]
        later[2 * j] = jnp.concatenate([x[:, :rank], x[:, :rank]], axis=1)
        later[2 * j + 1] = jnp.concatenate([x[:, rank:], x[:, rank:]], axis=1)
    now, later = later, now
    for load in loads[10:]:
        load.wait()
    near.wait()
    for h in range(2):
        for move in moves[h]:
            move.wait_send()
    cross_level(tgt_cross, now, near_in, later)
    now, later = later, now
    for depth in range(levels):
        local_level(tgt, depth, tgt_pair, now, later)
        now, later = later, now
    for b in range(blocks):
        y = jnp.dot(now[b][:, :rank], out_basis[b], preferred_element_type=F32)
        out_ref[:, b * points : (b + 1) * points] = y.astype(BF16)


def body(
    devices,
    vectors,
    leaf_basis,
    src_factors,
    src_cross,
    pair_factors,
    tgt_cross,
    tgt_factors,
    out_basis,
    src_pairing,
    tgt_pairing,
    pair_sources,
    pair_owner,
    pair_target,
):
    vec = vectors.shape[0]
    blocks, rank, _ = leaf_basis.shape
    pairs = pair_factors.shape[0]
    bits = devices.bit_length() - 1
    halves = blocks // 2
    width = 2 * rank
    rows = 4 + devices * blocks // pairs
    rows = -(-rows // 8) * 8
    small = [
        src_pairing,
        tgt_pairing,
        pair_sources.T,
        pair_owner.reshape(1, pairs),
        pair_target.reshape(1, pairs),
    ]
    big = [
        vectors,
        leaf_basis,
        src_factors,
        src_cross,
        pair_factors,
        tgt_cross,
        tgt_factors,
        out_basis,
    ]
    vmem = pl.BlockSpec(memory_space=pltpu.VMEM)
    hbm = pl.BlockSpec(memory_space=pltpu.HBM)
    rest = list(range(1, bits))
    orders = ([0] + rest, [0] + rest[len(rest) // 2 :] + rest[: len(rest) // 2])
    return pl.pallas_call(
        functools.partial(kernel, devices, orders),
        out_shape=jax.ShapeDtypeStruct(vectors.shape, BF16),
        in_specs=[hbm] * (len(small) + len(big)),
        out_specs=vmem,
        scratch_shapes=[pltpu.SMEM(a.shape, I32) for a in small[:2]]
        + [pltpu.VMEM(a.shape, a.dtype) for a in small[2:] + big]
        + [
            pltpu.VMEM((blocks, vec, width), BF16),
            pltpu.VMEM((blocks, vec, width), BF16),
            pltpu.VMEM((halves, vec, width), BF16),
            pltpu.VMEM((halves, vec, width), BF16),
            pltpu.VMEM((halves, vec, width), BF16),
            pltpu.VMEM((rows, pairs), I32),
            pltpu.SMEM((rows, pairs), I32),
            pltpu.VMEM((pairs + 1, vec, width), BF16),
            pltpu.VMEM((devices * halves, vec // 2, width), BF16),
            pltpu.VMEM((devices * halves, vec // 2, width), BF16),
            pltpu.VMEM((devices * halves, vec // 2, width), BF16),
            pltpu.VMEM((devices * halves, vec // 2, width), BF16),
            pltpu.SemaphoreType.DMA((len(small) + len(big),)),
            pltpu.SemaphoreType.DMA,
            pltpu.SemaphoreType.DMA((2 + 2 * bits,)),
            pltpu.SemaphoreType.DMA((2 + 2 * bits,)),
        ],
        compiler_params=pltpu.CompilerParams(
            collective_id=0, has_side_effects=True, vmem_limit_bytes=63 * 1024 * 1024
        ),
    )(
        *small,
        *big,
    )


def solution(mesh):
    in_specs = (
        P(None, ("grp", "leaf")),
        P(("grp", "leaf"), None, None),
        P(None, ("grp", "leaf"), None, None),
        P(("grp", "leaf"), None, None),
        P(("grp", "leaf"), None, None),
        P(("grp", "leaf"), None, None),
        P(None, ("grp", "leaf"), None, None),
        P(("grp", "leaf"), None, None),
        P(),
        P(),
        P(("grp", "leaf"), None),
        P(("grp", "leaf"), None),
        P(("grp", "leaf")),
    )
    out_specs = P(None, ("grp", "leaf"))
    return jax.shard_map(
        functools.partial(body, mesh.shape["leaf"]),
        mesh=mesh,
        in_specs=in_specs,
        out_specs=out_specs,
        check_vma=False,
    )
```
